128 devices in a mesh: dp: 16 (over x, z), mp: 8 (over y, core).
Axes of the slice: x: 4, y: 4, z: 4, core: 2. Of those that a mesh axis runs over, the one named last changes fastest.
Arguments:
- items: bfloat16 [131072, 256], P(('dp', 'mp')), may hold values from -32 to 32
- centroids: bfloat16 [8192, 256], replicated, may hold values from -2.5 to 2.5
Outputs:
- new_centroids: float32 [8192, 256], P(('dp', 'mp'))
- row_potential: float32 [131072], P(('dp', 'mp'))
- column_potential: float32 [8192], replicated
The draws below stay inside these ranges and needn't reach their ends.
All inputs are finite; a program needn't handle non-finite values.
Results may differ from the reference program's by a relative error of at most 0.0014.
Values sent between devices are 32-bit elements; how exact they have to be, the bound alone decides.
A program may use at most 128 MiB of HBM per device.

```python
import math
import jax
import jax.numpy as jnp
from jax import lax

D = 256
K = 8192
BALANCE_PASSES = 3
ITEMS = 131072


def shared_centroids(key):
    base_key, sign_key, size_key, pick_key = jax.random.split(key, 4)
    base = jnp.clip(jax.random.normal(base_key, (K, D), jnp.float32) * (4.0 / math.sqrt(D)), -1.2, 1.2)
    ranks = jax.random.permutation(pick_key, K)
    distant = (ranks < max(1, K // 64))[:, None]
    signs = jnp.where(jax.random.randint(sign_key, (K, D), 0, 2) == 0, -1.0, 1.0).astype(jnp.float32)
    sizes = jax.random.uniform(size_key, (K, D), jnp.float32, 2.2, 2.5)
    return (base, jnp.where(distant, signs * sizes, base))


def draw_centroids(key, part):
    base, whole = shared_centroids(key)
    return whole.astype(jnp.bfloat16)


def draw_items(key, part):
    base, whole = shared_centroids(key)
    key = jax.random.fold_in(key, 7)
    second = jax.random.fold_in(key, 1)
    third = jax.random.fold_in(key, 2)
    fourth = jax.random.fold_in(key, 3)
    value_entries = jax.random.normal(second, (ITEMS, D), jnp.float32)
    picks = jax.random.randint(third, (ITEMS,), 0, K)
    selected_centers = jnp.take(base, picks, axis=0)
    update_strength = jax.random.uniform(fourth, (ITEMS, 1), jnp.float32, 22.0, 26.0)
    flags = jax.random.randint(jax.random.fold_in(key, 5), (ITEMS, 1), 0, 64) == 0
    value_entries = jnp.where(flags, update_strength * selected_centers, value_entries)
    return jnp.clip(value_entries, -32.0, 32.0).astype(jnp.bfloat16)


def setup_inputs(seed: int = 0) -> dict:
    seeds = jax.random.split(jax.random.key(seed), 3)
    return {
        "items": draw_items(jax.random.fold_in(seeds[2], 71), 0),
        "centroids": draw_centroids(jax.random.fold_in(seeds[2], 71), 0),
    }


smoothing_divisor = 4.0


def compute_logits(block, centroids, length_powered):
    pairwise_similarity = lax.dot_general(block, centroids, (((1,), (1,)), ((), ())), preferred_element_type=jnp.float32)
    return (2.0 * pairwise_similarity - length_powered[None, :]) / smoothing_divisor


def reference(items, centroids):
    total, width = items.shape
    kcount = centroids.shape[0]
    block = min(4096, total)
    segment_list = items.reshape(total // block, block, width)
    cents32 = centroids.astype(jnp.float32)
    length_powered = jnp.einsum("kd,kd->k", cents32, cents32)
    target = jnp.log(jnp.float32(total) / jnp.float32(kcount))
    col_pot = jnp.zeros((kcount,), jnp.float32)
    row_pots = jnp.zeros((total // block, block), jnp.float32)
    for step in range(BALANCE_PASSES):
        def visit(carry, segment_length, col_pot=col_pot):
            peak, mass = carry
            assignment_scores = compute_logits(segment_length, centroids, length_powered)
            shifted = assignment_scores + col_pot[None, :]
            top = jnp.max(shifted, axis=1)
            row_pot = -(top + jnp.log(jnp.sum(jnp.exp(shifted - top[:, None]), axis=1)))
            moved = assignment_scores + row_pot[:, None]
            new_peak = jnp.maximum(peak, jnp.max(moved, axis=0))
            mass = mass * jnp.exp(peak - new_peak) + jnp.sum(jnp.exp(moved - new_peak[None, :]), axis=0)
            return (new_peak, mass), row_pot
        start = (jnp.full((kcount,), -jnp.inf, jnp.float32), jnp.zeros((kcount,), jnp.float32))
        (peak, mass), row_pots = lax.scan(visit, start, segment_list)
        col_pot = target - (peak + jnp.log(mass))

    def gather_running(acc, pair):
        segment_length, row_pot = pair
        assignment_scores = compute_logits(segment_length, centroids, length_powered)
        plan = jnp.exp(assignment_scores + row_pot[:, None] + col_pot[None, :]).astype(jnp.bfloat16)
        term = lax.dot_general(plan, segment_length, (((0,), (0,)), ((), ())), preferred_element_type=jnp.float32)
        return acc + term, None
    sums, unused = lax.scan(gather_running, jnp.zeros((kcount, width), jnp.float32), (segment_list, row_pots))
    new_centroids = (jnp.float32(kcount) / jnp.float32(total)) * sums
    return new_centroids, row_pots.reshape(total), col_pot
```

```python
import functools
import math

import jax
import jax.numpy as jnp
from jax import lax
from jax.experimental import pallas as pl
from jax.experimental.pallas import tpu as pltpu
from jax.sharding import PartitionSpec as P

MESH = pl.DeviceIdType.MESH
F32 = jnp.float32
BF16 = jnp.bfloat16
LOG2E = math.log2(math.e)
LN2 = math.log(2.0)
N = 1024
D = 256
CHIPS = 64
GROUPS = 8
ORDERS = (("x", "y", "z"), ("y", "z", "x"), ("z", "x", "y"))


def kernel(
    items_ref, cents_ref, out_ref, row_ref, col_ref,
    F, xt, wx, vec, peak, full, r1, r2, rd, ra1, rb1, ra2, rb2, r3, keep,
    ar_send, ar_recv, d_send, d_recv, a1_send, a1_recv, b1_send, b1_recv,
    a2_send, a2_recv, b2_send, b2_recv, c_send, c_recv,
):
    dp = lax.axis_index("dp")
    mp = lax.axis_index("mp")
    x, z = dp // 4, dp % 4
    y, core = mp // 2, mp % 2
    me = {"x": x, "y": y, "z": z}
    chip = x * 16 + z * 4 + y

    def device(axis, step):
        k = (me[axis] + step) % 4
        if axis == "x":
            return (k * 4 + z, mp)
        if axis == "z":
            return (x * 4 + k, mp)
        return (dp, k * 2 + core)

    barrier = pltpu.get_barrier_semaphore()
    for d in range(1, 8):
        pl.semaphore_signal(barrier, inc=1, device_id=(dp, (mp + d) % 8), device_id_type=MESH)
    for d in range(1, 16):
        pl.semaphore_signal(barrier, inc=1, device_id=((dp + d) % 16, mp), device_id_type=MESH)

    sends = []

    def remote(src, dst, send, recv, target):
        copy = pltpu.make_async_remote_copy(
            src_ref=src, dst_ref=dst, send_sem=send, recv_sem=recv,
            device_id=target, device_id_type=MESH,
        )
        copy.start()
        return copy

    def tree(parts, op):
        while len(parts) > 1:
            parts = [op(a, b) for a, b in zip(parts[::2], parts[1::2])] + (
                [parts[-1]] if len(parts) % 2 else []
            )
        return parts[0]

    def lane_tree(a, op):
        return tree([a[..., j * 128:(j + 1) * 128] for j in range(8)], op)

    xt[...] = items_ref[...].T
    rows1 = 512

    def first(i, carry):
        block = cents_ref[pl.ds(i * rows1, rows1), :]
        wide = block.astype(F32)
        sq = jnp.sum(wide * wide, axis=1, keepdims=True) * (0.25 * LOG2E)
        tops, sums = [], []
        for j in range(4):
            lanes = slice(j * 256, (j + 1) * 256)
            logit = jnp.dot(block, xt[:, lanes], preferred_element_type=F32)
            logit = logit * (0.5 * LOG2E) - sq
            F[pl.ds(i * (rows1 // 128), rows1 // 128), :, :, :, lanes] = logit.reshape(
                rows1 // 128, 2, 8, 8, 256
            )
            tiles = logit.reshape(rows1 // 8, 8, 256)
            top = jnp.maximum(carry[0][j], jnp.max(tiles, axis=0))
            total = carry[1][j] * jnp.exp2(carry[0][j] - top) + jnp.sum(
                jnp.exp2(tiles - top[None]), axis=0
            )
            tops.append(top)
            sums.append(total)
        return tuple(tops), tuple(sums)

    lows = tuple(jnp.full((8, 256), -jnp.inf, F32) for _ in range(4))
    zeros = tuple(jnp.zeros((8, 256), F32) for _ in range(4))
    tops, sums = lax.fori_loop(0, 8192 // rows1, first, (lows, zeros))
    top = jnp.concatenate(tops, axis=1)
    total = jnp.concatenate(sums, axis=1)
    best = jnp.max(top, axis=0, keepdims=True)
    total = jnp.sum(total * jnp.exp2(top - best), axis=0, keepdims=True)
    row1 = -(best + jnp.log2(total))
    keep[...] = jnp.broadcast_to(row1, (8, N))

    def second(i, _):
        a = F[i].reshape(16, 8, N)
        r = keep[...]
        p = None
        for j in range(8):
            lanes = slice(j * 128, (j + 1) * 128)
            m = a[:, :, lanes] + r[None, :, lanes]
            p = m if p is None else jnp.maximum(p, m)
        p = jnp.broadcast_to(jnp.max(p, axis=2, keepdims=True), (16, 8, 128))
        s = None
        for j in range(8):
            lanes = slice(j * 128, (j + 1) * 128)
            e = jnp.exp2(a[:, :, lanes] + r[None, :, lanes] - p)
            F[i, :, :, :, lanes] = e.reshape(2, 8, 8, 128)
            s = e if s is None else s + e
        p_row = p.reshape(128, 128).T[0:1, :]
        s_row = jnp.sum(s.reshape(128, 128).T, axis=0, keepdims=True)
        peak[pl.ds(i, 1), :] = p_row
        vec[0, pl.ds(i, 1), :] = p_row + jnp.log2(s_row)
        return 0

    lax.fori_loop(0, CHIPS, second, 0)

    pl.semaphore_wait(barrier, 22)

    def exchange(n, combine):
        own = pl.ds(mp * 8, 8)
        copies = []
        for d in range(1, 8):
            to = (mp + d) % 8
            copies.append(remote(
                vec.at[n, pl.ds(to * 8, 8)], r1.at[n, d - 1],
                ar_send.at[n, 0], ar_recv.at[n, 0], (dp, to),
            ))
        pltpu.make_async_copy(r1.at[n], r1.at[n], ar_recv.at[n, 0]).wait()
        part = combine([vec[n, own, :]] + [r1[n, d] for d in range(7)])
        r2[n, dp] = part
        for d in range(1, 16):
            remote(
                r2.at[n, dp], r2.at[n, dp],
                ar_send.at[n, 1], ar_recv.at[n, 1], ((dp + d) % 16, mp),
            )
        fifteen = r2.at[n, pl.ds(0, 15)]
        pltpu.make_async_copy(fifteen, fifteen, ar_recv.at[n, 1]).wait()
        full[n, own, :] = combine([r2[n, d] for d in range(16)])
        for d in range(1, 8):
            remote(
                full.at[n, own], full.at[n, own],
                ar_send.at[n, 2], ar_recv.at[n, 2], (dp, (mp + d) % 8),
            )
        pltpu.make_async_copy(r1.at[n], r1.at[n], ar_recv.at[n, 2]).wait()

    def exchange_sent(n):
        pltpu.make_async_copy(r1.at[n], r1.at[n], ar_send.at[n, 0]).wait()
        fifteen = r2.at[n, pl.ds(0, 15)]
        pltpu.make_async_copy(fifteen, fifteen, ar_send.at[n, 1]).wait()
        pltpu.make_async_copy(r1.at[n], r1.at[n], ar_send.at[n, 2]).wait()

    def logsum(parts):
        m = tree(parts, jnp.maximum)
        return m + jnp.log2(tree([jnp.exp2(a - m) for a in parts], jnp.add))

    def plainsum(parts):
        return tree(parts, jnp.add)

    def expand(rows_of):
        def body(i, _):
            wx[i] = jnp.broadcast_to(rows_of(i), (128, 128)).T
            return 0
        lax.fori_loop(0, CHIPS, body, 0)

    def row_sums():
        def body(i, carry):
            carry = list(carry)
            w = wx[i].reshape(16, 8, 128)
            for j in range(8):
                a = F[i, :, :, :, j * 128:(j + 1) * 128].reshape(16, 8, 128)
                carry[j] = carry[j] + jnp.sum(a * w, axis=0)
            return tuple(carry)
        zero = jnp.zeros((8, 128), F32)
        parts = lax.fori_loop(0, CHIPS, body, (zero,) * 8)
        return jnp.sum(jnp.concatenate(parts, axis=1), axis=0, keepdims=True)

    exchange(0, logsum)
    peak[...] = jnp.exp2(peak[...] + (4.0 - full[0]))

    expand(lambda i: peak[pl.ds(i, 1), :])
    keep2 = jnp.broadcast_to(1.0 / row_sums(), (8, N))

    def columns(n, u):
        def body(i, _):
            s = None
            for j in range(8):
                a = F[i, :, :, :, j * 128:(j + 1) * 128].reshape(16, 8, 128)
                a = a * u[None, :, j * 128:(j + 1) * 128]
                s = a if s is None else s + a
            s = jnp.sum(s.reshape(128, 128).T, axis=0, keepdims=True)
            vec[n, pl.ds(i, 1), :] = s * peak[pl.ds(i, 1), :]
            return 0
        lax.fori_loop(0, CHIPS, body, 0)

    columns(1, keep2)
    exchange(1, plainsum)
    peak[...] = peak[...] * (16.0 / full[1])

    expand(lambda i: peak[pl.ds(i, 1), :])
    rows3 = row_sums()
    row_ref[...] = LN2 * keep[0:1, :] - jnp.log(rows3)
    keep[...] = jnp.broadcast_to(1.0 / rows3, (8, N))
    columns(2, keep[...])
    exchange(2, plainsum)
    col_ref[...] = LN2 * ((12.0 - full[0]) - jnp.log2(full[1]) - jnp.log2(full[2]))
    peak[...] = peak[...] * (16.0 / full[2])
    expand(lambda i: peak[pl.ds(i, 1), :])

    def at(g, fixed, half=None):
        index = [g]
        first_free = True
        for axis in ("x", "z", "y"):
            if axis in fixed:
                index.append(fixed[axis])
            elif first_free:
                first_free = False
                index.append(slice(None) if half is None else pl.ds(half * 2, 2))
            else:
                index.append(slice(None))
        return tuple(index)

    copies = {}

    def product(g):
        w = wx[...].reshape(CHIPS, 2, 8, 8, 128)[:, :, g].reshape(128, 8, 128)
        parts = []
        for j in range(8):
            lanes = slice(j * 128, (j + 1) * 128)
            a = F[:, :, g, :, lanes].reshape(128, 8, 128) * (w * keep[:, lanes][None])
            parts.append(a.reshape(1024, 128).astype(BF16))
        plan = jnp.concatenate(parts, axis=1)
        sums = jnp.dot(plan, items_ref[...], preferred_element_type=F32)
        F[:, :, g, :, 0:256] = sums.reshape(CHIPS, 2, 8, 256)

    def pair_start(g):
        copies["d", g] = remote(
            F.at[:, 1 - core, g, :, 0:256], rd.at[g].reshape(CHIPS, 8, 256),
            d_send.at[g], d_recv.at[g], (dp, y * 2 + 1 - core),
        )

    def a_start(g, phase):
        order = ORDERS[g % 3]
        axis = order[phase]
        fixed = {a: me[a] for a in order[:phase]}
        fixed[axis] = (me[axis] + 2) % 4
        buf, send, recv = ((ra1, a1_send, a1_recv), (ra2, a2_send, a2_recv))[phase]
        for side, step in ((0, 1), (1, 3)):
            copies["a", phase, g, side] = remote(
                rd.at[at(g, fixed, side)], buf.at[g, side],
                send.at[g, side], recv.at[g, side], device(axis, step),
            )

    def a_finish(g, phase):
        order = ORDERS[g % 3]
        axis = order[phase]
        fixed = {a: me[a] for a in order[:phase]}
        buf = (ra1, ra2)[phase]
        for side, step in ((0, 1), (1, 3)):
            copies["a", phase, g, side].wait_recv()
            fixed[axis] = (me[axis] + step) % 4
            idx = at(g, fixed, side)
            rd[idx] = rd[idx] + buf[g, side]

    def b_start(g, phase):
        order = ORDERS[g % 3]
        axis = order[phase]
        fixed = {a: me[a] for a in order[:phase]}
        buf, send, recv = ((rb1, b1_send, b1_recv), (rb2, b2_send, b2_recv))[phase]
        for side, step in ((0, 1), (1, 3)):
            fixed[axis] = (me[axis] + step) % 4
            copies["b", phase, g, side] = remote(
                rd.at[at(g, fixed)], buf.at[g, side],
                send.at[g, side], recv.at[g, side], device(axis, step),
            )

    def b_finish(g, phase):
        order = ORDERS[g % 3]
        axis = order[phase]
        fixed = {a: me[a] for a in order[:phase]}
        fixed[axis] = me[axis]
        buf = (rb1, rb2)[phase]
        for side in (0, 1):
            copies["b", phase, g, side].wait_recv()
        idx = at(g, fixed)
        rd[idx] = rd[idx] + (buf[g, 0] + buf[g, 1])

    def c_start(g):
        order = ORDERS[g % 3]
        axis = order[2]
        fixed = {a: me[a] for a in order[:2]}
        for d in (1, 2, 3):
            fixed[axis] = (me[axis] + d) % 4
            copies["c", g, d] = remote(
                rd.at[at(g, fixed)], r3.at[g, d - 1],
                c_send.at[g, d - 1], c_recv.at[g, d - 1], device(axis, d),
            )

    def pair_finish(g):
        copies["d", g].wait_recv()
        own = F[:, core, g, :, 0:256].reshape(4, 4, 4, 8, 256)
        rd[g] = rd[g] + own

    for g in range(GROUPS + 3):
        if g < GROUPS:
            product(g)
            pair_start(g)
        if 1 <= g < GROUPS + 1:
            pair_finish(g - 1)
            a_start(g - 1, 0)
        if 3 <= g:
            a_finish(g - 3, 0)
            b_start(g - 3, 0)

    for g in range(GROUPS + 2):
        if g < GROUPS:
            b_finish(g, 0)
            a_start(g, 1)
        if g >= 2:
            a_finish(g - 2, 1)
            b_start(g - 2, 1)
    for g in range(GROUPS):
        b_finish(g, 1)
        c_start(g)
    for g in range(GROUPS):
        for d in (1, 2, 3):
            copies["c", g, d].wait_recv()
        total = rd[g, x, z, y] + (r3[g, 0] + (r3[g, 1] + r3[g, 2]))
        out_ref[g * 8:(g + 1) * 8, :] = total * (1.0 / 16.0)
    for n in range(3):
        exchange_sent(n)
    for copy in copies.values():
        copy.wait_send()


def shards(items, centroids):
    dma = pltpu.SemaphoreType.DMA
    vmem = pltpu.VMEM
    out, row, col = pl.pallas_call(
        kernel,
        out_shape=(
            jax.ShapeDtypeStruct((64, D), F32),
            jax.ShapeDtypeStruct((1, N), F32),
            jax.ShapeDtypeStruct((CHIPS, 128), F32),
        ),
        in_specs=[pl.BlockSpec(memory_space=pltpu.VMEM)] * 2,
        out_specs=[pl.BlockSpec(memory_space=pltpu.VMEM)] * 3,
        scratch_shapes=[
            vmem((CHIPS, 2, 8, 8, N), F32),
            vmem((D, N), BF16),
            vmem((CHIPS, 128, 128), F32),
            vmem((3, CHIPS, 128), F32),
            vmem((CHIPS, 128), F32),
            vmem((3, CHIPS, 128), F32),
            vmem((3, 7, 8, 128), F32),
            vmem((3, 16, 8, 128), F32),
            vmem((GROUPS, 4, 4, 4, 8, D), F32),
            vmem((GROUPS, 2, 2, 4, 8, D), F32),
            vmem((GROUPS, 2, 4, 4, 8, D), F32),
            vmem((GROUPS, 2, 2, 8, D), F32),
            vmem((GROUPS, 2, 4, 8, D), F32),
            vmem((GROUPS, 3, 8, D), F32),
            vmem((8, N), F32),
            dma((3, 3)), dma((3, 3)),
            dma((GROUPS,)), dma((GROUPS,)),
            dma((GROUPS, 2)), dma((GROUPS, 2)),
            dma((GROUPS, 2)), dma((GROUPS, 2)),
            dma((GROUPS, 2)), dma((GROUPS, 2)),
            dma((GROUPS, 2)), dma((GROUPS, 2)),
            dma((GROUPS, 3)), dma((GROUPS, 3)),
        ],
        compiler_params=pltpu.CompilerParams(
            collective_id=0, has_side_effects=True, vmem_limit_bytes=60 * 2**20
        ),
        name="sinkhorn_step",
    )(items, centroids)
    return out, row.reshape(N), col.reshape(8192)


def solution(mesh):
    return jax.shard_map(
        shards,
        mesh=mesh,
        in_specs=(P(("dp", "mp"), None), P()),
        out_specs=(P(("dp", "mp"), None), P(("dp", "mp")), P()),
        check_vma=False,
    )
```

```python
import functools
import math

import jax
import jax.numpy as jnp
from jax import lax
from jax.experimental import pallas as pl
from jax.experimental.pallas import tpu as pltpu
from jax.sharding import PartitionSpec as P

MESH = pl.DeviceIdType.MESH
F32 = jnp.float32
BF16 = jnp.bfloat16
TARGET = math.log(16.0)
N = 1024
D = 256
CHIPS = 64
GROUPS = 8
ORDERS = (("x", "y", "z"), ("y", "z", "x"), ("z", "x", "y"))


def kernel(
    items_ref, cents_ref, out_ref, row_ref, col_ref,
    F, xt, plan0, plan1, v0, v1, v2, full, r10, r11, r12, r20, r21, r22, rd, ra1, rb1, rb2, r3, keep,
    ar_send, ar_recv, d_send, d_recv, a1_send, a1_recv, b1_send, b1_recv,
    b2_send, b2_recv, c_send, c_recv,
):
    dp = lax.axis_index("dp")
    mp = lax.axis_index("mp")
    x, z = dp // 4, dp % 4
    y, core = mp // 2, mp % 2
    me = {"x": x, "y": y, "z": z}
    chip = x * 16 + z * 4 + y
    chips = F.reshape(CHIPS, 2, 8, 8, N)
    plans = (plan0, plan1)
    vecs, r1s, r2s = (v0, v1, v2), (r10, r11, r12), (r20, r21, r22)

    def device(axis, step):
        k = (me[axis] + step) % 4
        if axis == "x":
            return (k * 4 + z, mp)
        if axis == "z":
            return (x * 4 + k, mp)
        return (dp, k * 2 + core)

    barrier = pltpu.get_barrier_semaphore()
    for d in range(1, 8):
        pl.semaphore_signal(barrier, inc=1, device_id=(dp, (mp + d) % 8), device_id_type=MESH)
    for d in range(1, 16):
        pl.semaphore_signal(barrier, inc=1, device_id=((dp + d) % 16, mp), device_id_type=MESH)

    def remote(src, dst, send, recv, target):
        copy = pltpu.make_async_remote_copy(
            src_ref=src, dst_ref=dst, send_sem=send, recv_sem=recv,
            device_id=target, device_id_type=MESH,
        )
        copy.start()
        return copy

    def tree(parts, op):
        while len(parts) > 1:
            parts = [op(a, b) for a, b in zip(parts[::2], parts[1::2])] + (
                [parts[-1]] if len(parts) % 2 else []
            )
        return parts[0]

    def lane_tree(a, op):
        return tree([a[..., j * 128:(j + 1) * 128] for j in range(8)], op)

    xt[...] = items_ref[...].T
    rows1 = 512

    def first(i, carry):
        block = cents_ref[pl.ds(i * rows1, rows1), :]
        wide = block.astype(F32)
        wide = wide * wide
        wide = (wide[:, 0:128] + wide[:, 128:256]).T
        sq = wide[0:8]
        for k in range(1, 16):
            sq = sq + wide[k * 8:(k + 1) * 8]
        for k in (4, 2, 1):
            sq = sq + pltpu.roll(sq, k, 0)
        sq = jnp.concatenate([sq] * 16, axis=0).T * 0.25
        sq = jnp.concatenate([sq, sq], axis=1)
        tops, sums = [], []
        for j in range(4):
            lanes = slice(j * 256, (j + 1) * 256)
            logit = jnp.dot(block, xt[:, lanes], preferred_element_type=F32)
            logit = logit * 0.5 - sq
            tile0 = i * (rows1 // 8)
            F[tile0 // 128, pl.ds(tile0 % 128, rows1 // 8), :, lanes] = logit.reshape(
                rows1 // 8, 8, 256
            )
            tiles = logit.reshape(rows1 // 8, 8, 256)
            top = jnp.maximum(carry[0][j], jnp.max(tiles, axis=0))
            total = carry[1][j] * jnp.exp(carry[0][j] - top) + jnp.sum(
                jnp.exp(tiles - top[None]), axis=0
            )
            tops.append(top)
            sums.append(total)
        return tuple(tops), tuple(sums)

    lows = tuple(jnp.full((8, 256), -jnp.inf, F32) for _ in range(4))
    zeros = tuple(jnp.zeros((8, 256), F32) for _ in range(4))
    tops, sums = lax.fori_loop(0, 8192 // rows1, first, (lows, zeros))
    top = jnp.concatenate(tops, axis=1)
    total = jnp.concatenate(sums, axis=1)
    best = jnp.max(top, axis=0, keepdims=True)
    total = jnp.sum(total * jnp.exp(top - best), axis=0, keepdims=True)
    row1 = -(best + jnp.log(total))
    keep[...] = jnp.broadcast_to(row1, (8, N))

    lane = lax.broadcasted_iota(jnp.int32, (8, 128), 1)

    def spread(vector, t):
        return jnp.broadcast_to(vector[:, t:t + 1], (8, 128))

    def lane_sums(s):
        return jnp.broadcast_to(jnp.sum(s, axis=2, keepdims=True), s.shape)

    def collect(parts):
        out = jnp.zeros((8, 128), F32)
        for t in range(128):
            out = jnp.where(lane == t, parts[t // 8][t % 8], out)
        return out

    def second(i, _):
        b = (mp + 1 + i) % 8
        r = keep[...]
        peaks, sums = [], []
        for q in range(16):
            p = None
            for j in range(8):
                lanes = slice(j * 128, (j + 1) * 128)
                m = F[b, pl.ds(q * 8, 8), :, lanes] + r[None, :, lanes]
                p = m if p is None else jnp.maximum(p, m)
            peaks.append(jnp.broadcast_to(jnp.max(p, axis=2, keepdims=True), p.shape))
        for q in range(16):
            s = None
            for j in range(8):
                lanes = slice(j * 128, (j + 1) * 128)
                e = jnp.exp(F[b, pl.ds(q * 8, 8), :, lanes] + r[None, :, lanes] - peaks[q])
                s = e if s is None else s + e
            sums.append(lane_sums(s))
        vecs[0][b, 0] = collect(peaks)
        vecs[0][b, 1] = collect(sums)
        part_start(0, i, b)
        return 0

    def part_start(n, i, b):
        @pl.when(i < 7)
        def _():
            pltpu.make_async_remote_copy(
                src_ref=vecs[n].at[b], dst_ref=r1s[n].at[i],
                send_sem=ar_send.at[n, 0], recv_sem=ar_recv.at[n, 0],
                device_id=(dp, b), device_id_type=MESH,
            ).start()

    pl.semaphore_wait(barrier, 22)
    lax.fori_loop(0, 8, second, 0)

    def arrived(ref, sem):
        pltpu.make_async_copy(ref, ref, sem).wait()

    def exchange(n, combine, finish):
        r1, r2 = r1s[n], r2s[n]
        arrived(r1, ar_recv.at[n, 0])
        r2[dp] = combine([vecs[n][mp]] + [r1[d] for d in range(7)])
        for d in range(1, 16):
            remote(
                r2.at[dp], r2.at[dp],
                ar_send.at[n, 1], ar_recv.at[n, 1], ((dp + d) % 16, mp),
            )
        arrived(r2.at[pl.ds(0, 15)], ar_recv.at[n, 1])
        full[n, mp] = finish(combine([r2[d] for d in range(16)]))
        for d in range(1, 8):
            remote(
                full.at[n, mp], full.at[n, mp],
                ar_send.at[n, 2], ar_recv.at[n, 2], (dp, (mp + d) % 8),
            )
        arrived(full.at[n, pl.ds(0, 7)], ar_recv.at[n, 2])

    def exchange_sent(n):
        arrived(r1s[n], ar_send.at[n, 0])
        arrived(r2s[n].at[pl.ds(0, 15)], ar_send.at[n, 1])
        arrived(full.at[n, pl.ds(0, 7)], ar_send.at[n, 2])

    def logsum(parts):
        m = tree([a[0] for a in parts], jnp.maximum)
        total = tree([a[1] * jnp.exp(a[0] - m) for a in parts], jnp.add)
        return jnp.stack([m, total], 0)

    def plainsum(parts):
        return tree(parts, jnp.add)

    def row_sums(n):
        def body(b, carry):
            carry = list(carry)
            r = keep[...]
            c = full[n, b]
            for t in range(128):
                ct = spread(c, t)
                for j in range(8):
                    lanes = slice(j * 128, (j + 1) * 128)
                    carry[j] = carry[j] + jnp.exp(F[b, t, :, lanes] + ct + r[:, lanes])
            return tuple(carry)
        zero = jnp.zeros((8, 128), F32)
        parts = lax.fori_loop(0, 8, body, (zero,) * 8)
        return jnp.sum(jnp.concatenate(parts, axis=1), axis=0, keepdims=True)

    def columns(i, _, n):
        b = (mp + 1 + i) % 8
        r = keep[...]
        c = full[n - 1, b]
        sums = []
        for q in range(16):
            ct = jnp.stack([spread(c, q * 8 + k) for k in range(8)], 0)
            s = None
            for j in range(8):
                lanes = slice(j * 128, (j + 1) * 128)
                a = jnp.exp(F[b, pl.ds(q * 8, 8), :, lanes] + r[None, :, lanes] + ct)
                s = a if s is None else s + a
            sums.append(lane_sums(s))
        vecs[n][b, 0] = collect(sums)
        part_start(n, i, b)
        return 0

    exchange(0, logsum, lambda a: TARGET - (a[0] + jnp.log(a[1])))
    for n in (1, 2):
        row = keep[0:1, :] - jnp.log(row_sums(n - 1))
        keep[...] = jnp.broadcast_to(row, (8, N))
        lax.fori_loop(0, 8, functools.partial(columns, n=n), 0)
        exchange(n, plainsum, lambda a: TARGET - (jnp.log(a[0]) - full[n - 1, mp]))
    row_ref[...] = keep[0:1, :]
    col_ref[...] = full[2]

    def at(g, fixed, half=None):
        index = [g]
        first_free = True
        for axis in ("x", "z", "y"):
            if axis in fixed:
                index.append(fixed[axis])
            elif first_free:
                first_free = False
                index.append(slice(None) if half is None else pl.ds(half * 2, 2))
            else:
                index.append(slice(None))
        return tuple(index)

    copies = {}

    def product(g):
        plan = plans[g % 2]
        for b in range(8):
            c3 = full[2, b]
            ts = [c * 16 + k * 8 + g for c in range(8) for k in range(2)]
            ct = jnp.stack([spread(c3, t) for t in ts], 0)
            for j in range(8):
                lanes = slice(j * 128, (j + 1) * 128)
                a = jnp.stack([F[b, t, :, lanes] for t in ts], 0)
                a = jnp.exp(a + keep[:, lanes][None] + ct)
                plan[b * 128:(b + 1) * 128, lanes] = a.reshape(128, 128).astype(BF16)
        sums = jnp.dot(plan[...], items_ref[...], preferred_element_type=F32)
        chips[:, :, g, :, 0:256] = sums.reshape(CHIPS, 2, 8, 256)

    def pair_start(g):
        copies["d", g] = remote(
            chips.at[:, 1 - core, g, :, 0:256], rd.at[g].reshape(CHIPS, 8, 256),
            d_send.at[g], d_recv.at[g], (dp, y * 2 + 1 - core),
        )

    def a_start(g, phase):
        order = ORDERS[g % 3]
        axis = order[phase]
        fixed = {a: me[a] for a in order[:phase]}
        fixed[axis] = (me[axis] + 2) % 4
        buf, send, recv = (ra1, a1_send, a1_recv)
        for side, step in ((0, 1), (1, 3)):
            copies["a", phase, g, side] = remote(
                rd.at[at(g, fixed, side)], buf.at[g, side],
                send.at[g, side], recv.at[g, side], device(axis, step),
            )

    def a_finish(g, phase):
        order = ORDERS[g % 3]
        axis = order[phase]
        fixed = {a: me[a] for a in order[:phase]}
        buf = ra1
        for side, step in ((0, 1), (1, 3)):
            copies["a", phase, g, side].wait_recv()
            fixed[axis] = (me[axis] + step) % 4
            idx = at(g, fixed, side)
            rd[idx] = rd[idx] + buf[g, side]

    def b_start(g, phase):
        order = ORDERS[g % 3]
        axis = order[phase]
        fixed = {a: me[a] for a in order[:phase]}
        buf, send, recv = (rb1, b1_send, b1_recv)
        for side, step in ((0, 1), (1, 3)):
            fixed[axis] = (me[axis] + step) % 4
            copies["b", phase, g, side] = remote(
                rd.at[at(g, fixed)], buf.at[g, side],
                send.at[g, side], recv.at[g, side], device(axis, step),
            )

    def b_finish(g, phase):
        order = ORDERS[g % 3]
        axis = order[phase]
        fixed = {a: me[a] for a in order[:phase]}
        fixed[axis] = me[axis]
        buf = rb1
        for side in (0, 1):
            copies["b", phase, g, side].wait_recv()
        idx = at(g, fixed)
        rd[idx] = rd[idx] + (buf[g, 0] + buf[g, 1])

    def c_start(g, phase):
        order = ORDERS[g % 3]
        axis = order[phase]
        fixed = {a: me[a] for a in order[:phase]}
        buf, send, recv = ((rb2, b2_send, b2_recv), (r3, c_send, c_recv))[phase - 1]
        for d in (1, 2, 3):
            fixed[axis] = (me[axis] + d) % 4
            copies["c", phase, g, d] = remote(
                rd.at[at(g, fixed)], buf.at[g, d - 1],
                send.at[g, d - 1], recv.at[g, d - 1], device(axis, d),
            )

    def c_finish(g, phase):
        order = ORDERS[g % 3]
        fixed = {a: me[a] for a in order[:phase + 1]}
        buf = (rb2, r3)[phase - 1]
        for d in (1, 2, 3):
            copies["c", phase, g, d].wait_recv()
        return rd[at(g, fixed)] + (buf[g, 0] + (buf[g, 1] + buf[g, 2])), at(g, fixed)

    def pair_finish(g):
        copies["d", g].wait_recv()
        own = chips[:, core, g, :, 0:256].reshape(4, 4, 4, 8, 256)
        rd[g] = rd[g] + own

    for g in range(GROUPS + 3):
        if g < GROUPS:
            product(g)
            pair_start(g)
        if 1 <= g < GROUPS + 1:
            pair_finish(g - 1)
            a_start(g - 1, 0)
        if 3 <= g:
            a_finish(g - 3, 0)
            b_start(g - 3, 0)
    for g in range(GROUPS + 2):
        if g < GROUPS:
            b_finish(g, 0)
            c_start(g, 1)
        if g >= 2:
            total, index = c_finish(g - 2, 1)
            rd[index] = total
            c_start(g - 2, 2)
    for g in range(GROUPS):
        total, index = c_finish(g, 2)
        out_ref[g * 8:(g + 1) * 8, :] = total * (1.0 / 16.0)
    for n in range(3):
        exchange_sent(n)
    for copy in copies.values():
        copy.wait_send()


def shards(items, centroids):
    dma = pltpu.SemaphoreType.DMA
    vmem = pltpu.VMEM
    out, row, col = pl.pallas_call(
        kernel,
        out_shape=(
            jax.ShapeDtypeStruct((64, D), F32),
            jax.ShapeDtypeStruct((1, N), F32),
            jax.ShapeDtypeStruct((8, 8, 128), F32),
        ),
        in_specs=[pl.BlockSpec(memory_space=pltpu.VMEM)] * 2,
        out_specs=[pl.BlockSpec(memory_space=pltpu.VMEM)] * 3,
        scratch_shapes=[
            vmem((8, 128, 8, N), F32),
            vmem((D, N), BF16),
            vmem((N, N), BF16),
            vmem((N, N), BF16),
            vmem((8, 2, 8, 128), F32),
            vmem((8, 1, 8, 128), F32),
            vmem((8, 1, 8, 128), F32),
            vmem((3, 8, 8, 128), F32),
            vmem((7, 2, 8, 128), F32),
            vmem((7, 1, 8, 128), F32),
            vmem((7, 1, 8, 128), F32),
            vmem((16, 2, 8, 128), F32),
            vmem((16, 1, 8, 128), F32),
            vmem((16, 1, 8, 128), F32),
            vmem((GROUPS, 4, 4, 4, 8, D), F32),
            vmem((GROUPS, 2, 2, 4, 8, D), F32),
            vmem((GROUPS, 2, 4, 4, 8, D), F32),
            vmem((GROUPS, 3, 4, 8, D), F32),
            vmem((GROUPS, 3, 8, D), F32),
            vmem((8, N), F32),
            dma((3, 3)), dma((3, 3)),
            dma((GROUPS,)), dma((GROUPS,)),
            dma((GROUPS, 2)), dma((GROUPS, 2)),
            dma((GROUPS, 2)), dma((GROUPS, 2)),
            dma((GROUPS, 3)), dma((GROUPS, 3)),
            dma((GROUPS, 3)), dma((GROUPS, 3)),
        ],
        compiler_params=pltpu.CompilerParams(
            collective_id=0, has_side_effects=True, vmem_limit_bytes=60 * 2**20
        ),
        name="sinkhorn_step",
    )(items, centroids)
    return out, row.reshape(N), col.transpose(0, 2, 1).reshape(8192)


def solution(mesh):
    return jax.shard_map(
        shards,
        mesh=mesh,
        in_specs=(P(("dp", "mp"), None), P()),
        out_specs=(P(("dp", "mp"), None), P(("dp", "mp")), P()),
        check_vma=False,
    )
```

```python
import functools
import math

import jax
import jax.numpy as jnp
from jax import lax
from jax.experimental import pallas as pl
from jax.experimental.pallas import tpu as pltpu
from jax.sharding import PartitionSpec as P

MESH = pl.DeviceIdType.MESH
F32 = jnp.float32
BF16 = jnp.bfloat16
TARGET = math.log(16.0)
N = 1024
D = 256
CHIPS = 64
GROUPS = 8
ORDERS = (("x", "y", "z"), ("y", "z", "x"), ("z", "x", "y"))


def kernel(
    items_ref, cents_ref, out_ref, row_ref, col_ref,
    F, xt, cx, plan0, plan1, v0, v1, v2, full, r10, r11, r12, r20, r21, r22, rd, ra1, rb1, rb2, r3, keep,
    ar_send, ar_recv, d_send, d_recv, a1_send, a1_recv, b1_send, b1_recv,
    b2_send, b2_recv, c_send, c_recv,
):
    dp = lax.axis_index("dp")
    mp = lax.axis_index("mp")
    x, z = dp // 4, dp % 4
    y, core = mp // 2, mp % 2
    me = {"x": x, "y": y, "z": z}
    chip = x * 16 + z * 4 + y
    chips = F.reshape(CHIPS, 2, 8, 8, N)
    plans = (plan0, plan1)
    vecs, r1s, r2s = (v0, v1, v2), (r10, r11, r12), (r20, r21, r22)

    def device(axis, step):
        k = (me[axis] + step) % 4
        if axis == "x":
            return (k * 4 + z, mp)
        if axis == "z":
            return (x * 4 + k, mp)
        return (dp, k * 2 + core)

    barrier = pltpu.get_barrier_semaphore()
    for d in range(1, 8):
        pl.semaphore_signal(barrier, inc=1, device_id=(dp, (mp + d) % 8), device_id_type=MESH)
    for d in range(1, 16):
        pl.semaphore_signal(barrier, inc=1, device_id=((dp + d) % 16, mp), device_id_type=MESH)

    def remote(src, dst, send, recv, target):
        copy = pltpu.make_async_remote_copy(
            src_ref=src, dst_ref=dst, send_sem=send, recv_sem=recv,
            device_id=target, device_id_type=MESH,
        )
        copy.start()
        return copy

    def tree(parts, op):
        while len(parts) > 1:
            parts = [op(a, b) for a, b in zip(parts[::2], parts[1::2])] + (
                [parts[-1]] if len(parts) % 2 else []
            )
        return parts[0]

    def lane_tree(a, op):
        return tree([a[..., j * 128:(j + 1) * 128] for j in range(8)], op)

    xt[...] = items_ref[...].T
    rows1 = 512

    def first(i, carry):
        block = cents_ref[pl.ds(i * rows1, rows1), :]
        wide = block.astype(F32)
        wide = wide * wide
        wide = (wide[:, 0:128] + wide[:, 128:256]).T
        sq = wide[0:8]
        for k in range(1, 16):
            sq = sq + wide[k * 8:(k + 1) * 8]
        for k in (4, 2, 1):
            sq = sq + pltpu.roll(sq, k, 0)
        sq = jnp.concatenate([sq] * 16, axis=0).T * 0.25
        sq = jnp.concatenate([sq, sq], axis=1)
        tops, sums = [], []
        for j in range(4):
            lanes = slice(j * 256, (j + 1) * 256)
            logit = jnp.dot(block, xt[:, lanes], preferred_element_type=F32)
            logit = logit * 0.5 - sq
            tile0 = i * (rows1 // 8)
            F[tile0 // 128, pl.ds(tile0 % 128, rows1 // 8), :, lanes] = logit.reshape(
                rows1 // 8, 8, 256
            )
            tiles = logit.reshape(rows1 // 8, 8, 256)
            top = jnp.maximum(carry[0][j], jnp.max(tiles, axis=0))
            total = carry[1][j] * jnp.exp(carry[0][j] - top) + jnp.sum(
                jnp.exp(tiles - top[None]), axis=0
            )
            tops.append(top)
            sums.append(total)
        return tuple(tops), tuple(sums)

    lows = tuple(jnp.full((8, 256), -jnp.inf, F32) for _ in range(4))
    zeros = tuple(jnp.zeros((8, 256), F32) for _ in range(4))
    tops, sums = lax.fori_loop(0, 8192 // rows1, first, (lows, zeros))
    top = jnp.concatenate(tops, axis=1)
    total = jnp.concatenate(sums, axis=1)
    best = jnp.max(top, axis=0, keepdims=True)
    total = jnp.sum(total * jnp.exp(top - best), axis=0, keepdims=True)
    row1 = -(best + jnp.log(total))
    keep[...] = jnp.broadcast_to(row1, (8, N))

    lane = lax.broadcasted_iota(jnp.int32, (8, 128), 1)

    def spread(vector, t):
        return jnp.broadcast_to(vector[:, t:t + 1], (8, 128))

    def lane_sums(s):
        return jnp.broadcast_to(jnp.sum(s, axis=2, keepdims=True), s.shape)

    def collect(parts):
        out = jnp.zeros((8, 128), F32)
        for t in range(128):
            out = jnp.where(lane == t, parts[t // 8][t % 8], out)
        return out

    def second(i, _):
        b = (mp + 1 + i) % 8
        r = keep[...]
        peaks, sums = [], []
        for q in range(16):
            p = None
            for j in range(8):
                lanes = slice(j * 128, (j + 1) * 128)
                m = F[b, pl.ds(q * 8, 8), :, lanes] + r[None, :, lanes]
                p = m if p is None else jnp.maximum(p, m)
            peaks.append(jnp.broadcast_to(jnp.max(p, axis=2, keepdims=True), p.shape))
        for q in range(16):
            s = None
            for j in range(8):
                lanes = slice(j * 128, (j + 1) * 128)
                e = jnp.exp(F[b, pl.ds(q * 8, 8), :, lanes] + r[None, :, lanes] - peaks[q])
                s = e if s is None else s + e
            sums.append(lane_sums(s))
        vecs[0][b, 0] = collect(peaks)
        vecs[0][b, 1] = collect(sums)
        part_start(0, i, b)
        return 0

    def part_start(n, i, b):
        @pl.when(i < 7)
        def _():
            pltpu.make_async_remote_copy(
                src_ref=vecs[n].at[b], dst_ref=r1s[n].at[i],
                send_sem=ar_send.at[n, 0], recv_sem=ar_recv.at[n, 0],
                device_id=(dp, b), device_id_type=MESH,
            ).start()

    pl.semaphore_wait(barrier, 22)
    lax.fori_loop(0, 8, second, 0)

    def arrived(ref, sem):
        pltpu.make_async_copy(ref, ref, sem).wait()

    def exchange(n, combine, finish):
        r1, r2 = r1s[n], r2s[n]
        arrived(r1, ar_recv.at[n, 0])
        r2[dp] = combine([vecs[n][mp]] + [r1[d] for d in range(7)])
        for d in range(1, 16):
            remote(
                r2.at[dp], r2.at[dp],
                ar_send.at[n, 1], ar_recv.at[n, 1], ((dp + d) % 16, mp),
            )
        arrived(r2.at[pl.ds(0, 15)], ar_recv.at[n, 1])
        full[n, mp] = finish(combine([r2[d] for d in range(16)]))
        for d in range(1, 8):
            remote(
                full.at[n, mp], full.at[n, mp],
                ar_send.at[n, 2], ar_recv.at[n, 2], (dp, (mp + d) % 8),
            )
        arrived(full.at[n, pl.ds(0, 7)], ar_recv.at[n, 2])

    def exchange_sent(n):
        arrived(r1s[n], ar_send.at[n, 0])
        arrived(r2s[n].at[pl.ds(0, 15)], ar_send.at[n, 1])
        arrived(full.at[n, pl.ds(0, 7)], ar_send.at[n, 2])

    def logsum(parts):
        m = tree([a[0] for a in parts], jnp.maximum)
        total = tree([a[1] * jnp.exp(a[0] - m) for a in parts], jnp.add)
        return jnp.stack([m, total], 0)

    def plainsum(parts):
        return tree(parts, jnp.add)

    def row_sums(n):
        def body(b, carry):
            carry = list(carry)
            r = keep[...]
            c = full[n, b]
            for t in range(128):
                ct = spread(c, t)
                cx[b, t] = ct
                for j in range(8):
                    lanes = slice(j * 128, (j + 1) * 128)
                    carry[j] = carry[j] + jnp.exp(F[b, t, :, lanes] + ct + r[:, lanes])
            return tuple(carry)
        zero = jnp.zeros((8, 128), F32)
        parts = lax.fori_loop(0, 8, body, (zero,) * 8)
        return jnp.sum(jnp.concatenate(parts, axis=1), axis=0, keepdims=True)

    def columns(i, _, n):
        b = (mp + 1 + i) % 8
        r = keep[...]
        sums = []
        for q in range(16):
            ct = cx[b, pl.ds(q * 8, 8)]
            s = None
            for j in range(8):
                lanes = slice(j * 128, (j + 1) * 128)
                a = jnp.exp(F[b, pl.ds(q * 8, 8), :, lanes] + r[None, :, lanes] + ct)
                s = a if s is None else s + a
            sums.append(lane_sums(s))
        vecs[n][b, 0] = collect(sums)
        part_start(n, i, b)
        return 0

    exchange(0, logsum, lambda a: TARGET - (a[0] + jnp.log(a[1])))
    for n in (1, 2):
        row = keep[0:1, :] - jnp.log(row_sums(n - 1))
        keep[...] = jnp.broadcast_to(row, (8, N))
        lax.fori_loop(0, 8, functools.partial(columns, n=n), 0)
        exchange(n, plainsum, lambda a: TARGET - (jnp.log(a[0]) - full[n - 1, mp]))
    row_ref[...] = keep[0:1, :]
    col_ref[...] = full[2]

    def at(g, fixed, half=None):
        index = [g]
        first_free = True
        for axis in ("x", "z", "y"):
            if axis in fixed:
                index.append(fixed[axis])
            elif first_free:
                first_free = False
                index.append(slice(None) if half is None else pl.ds(half * 2, 2))
            else:
                index.append(slice(None))
        return tuple(index)

    copies = {}

    def product(g):
        plan = plans[g % 2]
        for b in range(8):
            c3 = full[2, b]
            ts = [c * 16 + k * 8 + g for c in range(8) for k in range(2)]
            ct = jnp.stack([spread(c3, t) for t in ts], 0)
            for j in range(8):
                lanes = slice(j * 128, (j + 1) * 128)
                a = jnp.stack([F[b, t, :, lanes] for t in ts], 0)
                a = jnp.exp(a + keep[:, lanes][None] + ct)
                plan[b * 128:(b + 1) * 128, lanes] = a.reshape(128, 128).astype(BF16)
        sums = jnp.dot(plan[...], items_ref[...], preferred_element_type=F32)
        chips[:, :, g, :, 0:256] = sums.reshape(CHIPS, 2, 8, 256)

    def pair_start(g):
        copies["d", g] = remote(
            chips.at[:, 1 - core, g, :, 0:256], rd.at[g].reshape(CHIPS, 8, 256),
            d_send.at[g], d_recv.at[g], (dp, y * 2 + 1 - core),
        )

    def a_start(g, phase):
        order = ORDERS[g % 3]
        axis = order[phase]
        fixed = {a: me[a] for a in order[:phase]}
        fixed[axis] = (me[axis] + 2) % 4
        buf, send, recv = (ra1, a1_send, a1_recv)
        for side, step in ((0, 1), (1, 3)):
            copies["a", phase, g, side] = remote(
                rd.at[at(g, fixed, side)], buf.at[g, side],
                send.at[g, side], recv.at[g, side], device(axis, step),
            )

    def a_finish(g, phase):
        order = ORDERS[g % 3]
        axis = order[phase]
        fixed = {a: me[a] for a in order[:phase]}
        buf = ra1
        for side, step in ((0, 1), (1, 3)):
            copies["a", phase, g, side].wait_recv()
            fixed[axis] = (me[axis] + step) % 4
            idx = at(g, fixed, side)
            rd[idx] = rd[idx] + buf[g, side]

    def b_start(g, phase):
        order = ORDERS[g % 3]
        axis = order[phase]
        fixed = {a: me[a] for a in order[:phase]}
        buf, send, recv = (rb1, b1_send, b1_recv)
        for side, step in ((0, 1), (1, 3)):
            fixed[axis] = (me[axis] + step) % 4
            copies["b", phase, g, side] = remote(
                rd.at[at(g, fixed)], buf.at[g, side],
                send.at[g, side], recv.at[g, side], device(axis, step),
            )

    def b_finish(g, phase):
        order = ORDERS[g % 3]
        axis = order[phase]
        fixed = {a: me[a] for a in order[:phase]}
        fixed[axis] = me[axis]
        buf = rb1
        for side in (0, 1):
            copies["b", phase, g, side].wait_recv()
        idx = at(g, fixed)
        rd[idx] = rd[idx] + (buf[g, 0] + buf[g, 1])

    def c_start(g, phase):
        order = ORDERS[g % 3]
        axis = order[phase]
        fixed = {a: me[a] for a in order[:phase]}
        buf, send, recv = ((rb2, b2_send, b2_recv), (r3, c_send, c_recv))[phase - 1]
        for d in (1, 2, 3):
            fixed[axis] = (me[axis] + d) % 4
            copies["c", phase, g, d] = remote(
                rd.at[at(g, fixed)], buf.at[g, d - 1],
                send.at[g, d - 1], recv.at[g, d - 1], device(axis, d),
            )

    def c_finish(g, phase):
        order = ORDERS[g % 3]
        fixed = {a: me[a] for a in order[:phase + 1]}
        buf = (rb2, r3)[phase - 1]
        for d in (1, 2, 3):
            copies["c", phase, g, d].wait_recv()
        return rd[at(g, fixed)] + (buf[g, 0] + (buf[g, 1] + buf[g, 2])), at(g, fixed)

    def pair_finish(g):
        copies["d", g].wait_recv()
        own = chips[:, core, g, :, 0:256].reshape(4, 4, 4, 8, 256)
        rd[g] = rd[g] + own

    for g in range(GROUPS + 3):
        if g < GROUPS:
            product(g)
            pair_start(g)
        if 1 <= g < GROUPS + 1:
            pair_finish(g - 1)
            a_start(g - 1, 0)
        if 3 <= g:
            a_finish(g - 3, 0)
            b_start(g - 3, 0)
    for g in range(GROUPS + 2):
        if g < GROUPS:
            b_finish(g, 0)
            c_start(g, 1)
        if g >= 2:
            total, index = c_finish(g - 2, 1)
            rd[index] = total
            c_start(g - 2, 2)
    for g in range(GROUPS):
        total, index = c_finish(g, 2)
        out_ref[g * 8:(g + 1) * 8, :] = total * (1.0 / 16.0)
    for n in range(3):
        exchange_sent(n)
    for copy in copies.values():
        copy.wait_send()


def shards(items, centroids):
    dma = pltpu.SemaphoreType.DMA
    vmem = pltpu.VMEM
    out, row, col = pl.pallas_call(
        kernel,
        out_shape=(
            jax.ShapeDtypeStruct((64, D), F32),
            jax.ShapeDtypeStruct((1, N), F32),
            jax.ShapeDtypeStruct((8, 8, 128), F32),
        ),
        in_specs=[pl.BlockSpec(memory_space=pltpu.VMEM)] * 2,
        out_specs=[pl.BlockSpec(memory_space=pltpu.VMEM)] * 3,
        scratch_shapes=[
            vmem((8, 128, 8, N), F32),
            vmem((D, N), BF16),
            vmem((8, 128, 8, 128), F32),
            vmem((N, N), BF16),
            vmem((N, N), BF16),
            vmem((8, 2, 8, 128), F32),
            vmem((8, 1, 8, 128), F32),
            vmem((8, 1, 8, 128), F32),
            vmem((3, 8, 8, 128), F32),
            vmem((7, 2, 8, 128), F32),
            vmem((7, 1, 8, 128), F32),
            vmem((7, 1, 8, 128), F32),
            vmem((16, 2, 8, 128), F32),
            vmem((16, 1, 8, 128), F32),
            vmem((16, 1, 8, 128), F32),
            vmem((GROUPS, 4, 4, 4, 8, D), F32),
            vmem((GROUPS, 2, 2, 4, 8, D), F32),
            vmem((GROUPS, 2, 4, 4, 8, D), F32),
            vmem((GROUPS, 3, 4, 8, D), F32),
            vmem((GROUPS, 3, 8, D), F32),
            vmem((8, N), F32),
            dma((3, 3)), dma((3, 3)),
            dma((GROUPS,)), dma((GROUPS,)),
            dma((GROUPS, 2)), dma((GROUPS, 2)),
            dma((GROUPS, 2)), dma((GROUPS, 2)),
            dma((GROUPS, 3)), dma((GROUPS, 3)),
            dma((GROUPS, 3)), dma((GROUPS, 3)),
        ],
        compiler_params=pltpu.CompilerParams(
            collective_id=0, has_side_effects=True, vmem_limit_bytes=60 * 2**20
        ),
        name="sinkhorn_step",
    )(items, centroids)
    return out, row.reshape(N), col.transpose(0, 2, 1).reshape(8192)


def solution(mesh):
    return jax.shard_map(
        shards,
        mesh=mesh,
        in_specs=(P(("dp", "mp"), None), P()),
        out_specs=(P(("dp", "mp"), None), P(("dp", "mp")), P()),
        check_vma=False,
    )
```

```python
import functools
import math

import jax
import jax.numpy as jnp
from jax import lax
from jax.experimental import pallas as pl
from jax.experimental.pallas import tpu as pltpu
from jax.sharding import PartitionSpec as P

MESH = pl.DeviceIdType.MESH
F32 = jnp.float32
BF16 = jnp.bfloat16
TARGET = math.log(16.0)
N = 1024
D = 256
CHIPS = 64
GROUPS = 8
SLOT = (0, 3, 6, 1, 4, 7, 2, 5)
ORDERS = (("x", "y", "z"), ("y", "z", "x"), ("z", "x", "y"))


def kernel(
    items_ref, cents_ref, out_ref, row_ref, col_ref,
    F, xt, cx, plan0, plan1, v0, v1, v2, full, r10, r11, r12, r20, r21, r22, rd, ra1, rb1, rb2, r3, keep,
    ar_send, ar_recv, d_send, d_recv, a1_send, a1_recv, b1_send, b1_recv,
    b2_send, b2_recv, c_send, c_recv,
):
    dp = lax.axis_index("dp")
    mp = lax.axis_index("mp")
    x, z = dp // 4, dp % 4
    y, core = mp // 2, mp % 2
    me = {"x": x, "y": y, "z": z}
    chip = x * 16 + z * 4 + y
    plans = (plan0, plan1)
    halves = cx.reshape(4, 2, CHIPS, 8, D)
    vecs, r1s, r2s = (v0, v1, v2), (r10, r11, r12), (r20, r21, r22)

    def device(axis, step):
        k = (me[axis] + step) % 4
        if axis == "x":
            return (k * 4 + z, mp)
        if axis == "z":
            return (x * 4 + k, mp)
        return (dp, k * 2 + core)

    barrier = pltpu.get_barrier_semaphore()
    for d in range(1, 8):
        pl.semaphore_signal(barrier, inc=1, device_id=(dp, (mp + d) % 8), device_id_type=MESH)
    for d in range(1, 16):
        pl.semaphore_signal(barrier, inc=1, device_id=((dp + d) % 16, mp), device_id_type=MESH)

    def remote(src, dst, send, recv, target):
        copy = pltpu.make_async_remote_copy(
            src_ref=src, dst_ref=dst, send_sem=send, recv_sem=recv,
            device_id=target, device_id_type=MESH,
        )
        copy.start()
        return copy

    def tree(parts, op):
        while len(parts) > 1:
            parts = [op(a, b) for a, b in zip(parts[::2], parts[1::2])] + (
                [parts[-1]] if len(parts) % 2 else []
            )
        return parts[0]

    def lane_tree(a, op):
        return tree([a[..., j * 128:(j + 1) * 128] for j in range(8)], op)

    xt[...] = items_ref[...].T
    rows1 = 512

    def first(i, carry):
        block = cents_ref[pl.ds(i * rows1, rows1), :]
        wide = block.astype(F32)
        wide = wide * wide
        wide = (wide[:, 0:128] + wide[:, 128:256]).T
        sq = wide[0:8]
        for k in range(1, 16):
            sq = sq + wide[k * 8:(k + 1) * 8]
        for k in (4, 2, 1):
            sq = sq + pltpu.roll(sq, k, 0)
        sq = jnp.concatenate([sq] * 16, axis=0).T * 0.25
        sq = jnp.concatenate([sq, sq], axis=1)
        tops, sums = [], []
        for j in range(4):
            lanes = slice(j * 256, (j + 1) * 256)
            logit = jnp.dot(block, xt[:, lanes], preferred_element_type=F32)
            logit = logit * 0.5 - sq
            tile0 = i * (rows1 // 8)
            F[tile0 // 128, pl.ds(tile0 % 128, rows1 // 8), :, lanes] = logit.reshape(
                rows1 // 8, 8, 256
            )
            tiles = logit.reshape(rows1 // 8, 8, 256)
            top = jnp.maximum(carry[0][j], jnp.max(tiles, axis=0))
            total = carry[1][j] * jnp.exp(carry[0][j] - top) + jnp.sum(
                jnp.exp(tiles - top[None]), axis=0
            )
            tops.append(top)
            sums.append(total)
        return tuple(tops), tuple(sums)

    lows = tuple(jnp.full((8, 256), -jnp.inf, F32) for _ in range(4))
    zeros = tuple(jnp.zeros((8, 256), F32) for _ in range(4))
    tops, sums = lax.fori_loop(0, 8192 // rows1, first, (lows, zeros))
    top = jnp.concatenate(tops, axis=1)
    total = jnp.concatenate(sums, axis=1)
    best = jnp.max(top, axis=0, keepdims=True)
    total = jnp.sum(total * jnp.exp(top - best), axis=0, keepdims=True)
    row1 = -(best + jnp.log(total))
    keep[...] = jnp.broadcast_to(row1, (8, N))

    lane = lax.broadcasted_iota(jnp.int32, (8, 128), 1)

    def spread(vector, t):
        return jnp.broadcast_to(vector[:, t:t + 1], (8, 128))

    def lane_sums(s):
        return jnp.broadcast_to(jnp.sum(s, axis=2, keepdims=True), s.shape)

    def collect(parts):
        out = jnp.zeros((8, 128), F32)
        for t in range(128):
            out = jnp.where(lane == t, parts[t // 8][t % 8], out)
        return out

    def second(i, _):
        b = (mp + 1 + i) % 8
        r = keep[...]
        peaks, sums = [], []
        for q in range(16):
            p = None
            for j in range(8):
                lanes = slice(j * 128, (j + 1) * 128)
                m = F[b, pl.ds(q * 8, 8), :, lanes] + r[None, :, lanes]
                p = m if p is None else jnp.maximum(p, m)
            peaks.append(jnp.broadcast_to(jnp.max(p, axis=2, keepdims=True), p.shape))
        for q in range(16):
            s = None
            for j in range(8):
                lanes = slice(j * 128, (j + 1) * 128)
                e = jnp.exp(F[b, pl.ds(q * 8, 8), :, lanes] + r[None, :, lanes] - peaks[q])
                s = e if s is None else s + e
            sums.append(lane_sums(s))
        vecs[0][b, 0] = collect(peaks)
        vecs[0][b, 1] = collect(sums)
        part_start(0, i, b)
        return 0

    def part_start(n, i, b):
        @pl.when(i < 7)
        def _():
            pltpu.make_async_remote_copy(
                src_ref=vecs[n].at[b], dst_ref=r1s[n].at[i],
                send_sem=ar_send.at[n, 0], recv_sem=ar_recv.at[n, 0],
                device_id=(dp, b), device_id_type=MESH,
            ).start()

    pl.semaphore_wait(barrier, 22)
    lax.fori_loop(0, 8, second, 0)

    def arrived(ref, sem):
        pltpu.make_async_copy(ref, ref, sem).wait()

    def exchange(n, combine, finish):
        r1, r2 = r1s[n], r2s[n]
        arrived(r1, ar_recv.at[n, 0])
        r2[dp] = combine([vecs[n][mp]] + [r1[d] for d in range(7)])
        for d in range(1, 16):
            remote(
                r2.at[dp], r2.at[dp],
                ar_send.at[n, 1], ar_recv.at[n, 1], ((dp + d) % 16, mp),
            )
        arrived(r2.at[pl.ds(0, 15)], ar_recv.at[n, 1])
        full[n, mp] = finish(combine([r2[d] for d in range(16)]))
        for d in range(1, 8):
            remote(
                full.at[n, mp], full.at[n, mp],
                ar_send.at[n, 2], ar_recv.at[n, 2], (dp, (mp + d) % 8),
            )
        arrived(full.at[n, pl.ds(0, 7)], ar_recv.at[n, 2])

    def exchange_sent(n):
        arrived(r1s[n], ar_send.at[n, 0])
        arrived(r2s[n].at[pl.ds(0, 15)], ar_send.at[n, 1])
        arrived(full.at[n, pl.ds(0, 7)], ar_send.at[n, 2])

    def logsum(parts):
        m = tree([a[0] for a in parts], jnp.maximum)
        total = tree([a[1] * jnp.exp(a[0] - m) for a in parts], jnp.add)
        return jnp.stack([m, total], 0)

    def plainsum(parts):
        return tree(parts, jnp.add)

    def row_sums(n):
        def body(b, carry):
            carry = list(carry)
            r = keep[...]
            c = full[n, b]
            for t in range(128):
                ct = spread(c, t)
                cx[b, t // 2, :, t % 2 * 128:(t % 2 + 1) * 128] = ct
                for j in range(8):
                    lanes = slice(j * 128, (j + 1) * 128)
                    carry[j] = carry[j] + jnp.exp(F[b, t, :, lanes] + ct + r[:, lanes])
            return tuple(carry)
        zero = jnp.zeros((8, 128), F32)
        parts = lax.fori_loop(0, 8, body, (zero,) * 8)
        return jnp.sum(jnp.concatenate(parts, axis=1), axis=0, keepdims=True)

    def columns(i, _, n):
        b = (mp + 1 + i) % 8
        r = keep[...]
        sums = []
        for q in range(16):
            ct = jnp.stack([cx[b, q * 4 + k // 2, :, k % 2 * 128:(k % 2 + 1) * 128] for k in range(8)], 0)
            s = None
            for j in range(8):
                lanes = slice(j * 128, (j + 1) * 128)
                a = jnp.exp(F[b, pl.ds(q * 8, 8), :, lanes] + r[None, :, lanes] + ct)
                s = a if s is None else s + a
            sums.append(lane_sums(s))
        vecs[n][b, 0] = collect(sums)
        part_start(n, i, b)
        return 0

    exchange(0, logsum, lambda a: TARGET - (a[0] + jnp.log(a[1])))
    for n in (1, 2):
        row = keep[0:1, :] - jnp.log(row_sums(n - 1))
        keep[...] = jnp.broadcast_to(row, (8, N))
        lax.fori_loop(0, 8, functools.partial(columns, n=n), 0)
        exchange(n, plainsum, lambda a: TARGET - (jnp.log(a[0]) - full[n - 1, mp]))
    row_ref[...] = keep[0:1, :]
    col_ref[...] = full[2]

    def at(g, fixed, half=None):
        index = [SLOT[g] if isinstance(g, int) else g]
        first_free = True
        for axis in ("x", "z", "y"):
            if axis in fixed:
                index.append(fixed[axis])
            elif first_free:
                first_free = False
                index.append(slice(None) if half is None else pl.ds(half * 2, 2))
            else:
                index.append(slice(None))
        return tuple(index)

    copies = {}

    def product(g):
        plan = plans[g % 2]
        for b in range(8):
            c3 = full[2, b]
            ts = [c * 16 + k * 8 + g for c in range(8) for k in range(2)]
            ct = jnp.stack([spread(c3, t) for t in ts], 0)
            for j in range(8):
                lanes = slice(j * 128, (j + 1) * 128)
                a = jnp.stack([F[b, t, :, lanes] for t in ts], 0)
                a = jnp.exp(a + keep[:, lanes][None] + ct)
                plan[b * 128:(b + 1) * 128, lanes] = a.reshape(128, 128).astype(BF16)
        sums = jnp.dot(plan[...], items_ref[...], preferred_element_type=F32)
        if g >= 4:
            copies["d", g - 4].wait_send()
        sums = sums.reshape(CHIPS, 2, 8, 256)
        halves[g % 4, 0] = sums[:, 0]
        halves[g % 4, 1] = sums[:, 1]

    def pair_start(g):
        copies["d", g] = remote(
            halves.at[g % 4, 1 - core], rd.at[SLOT[g]].reshape(CHIPS, 8, 256),
            d_send.at[g], d_recv.at[g], (dp, y * 2 + 1 - core),
        )

    def a_start(g, phase):
        order = ORDERS[g % 3]
        axis = order[phase]
        fixed = {a: me[a] for a in order[:phase]}
        fixed[axis] = (me[axis] + 2) % 4
        buf, send, recv = (ra1, a1_send, a1_recv)
        for side, step in ((0, 1), (1, 3)):
            copies["a", phase, g, side] = remote(
                rd.at[at(g, fixed, side)], buf.at[g, side],
                send.at[g, side], recv.at[g, side], device(axis, step),
            )

    def a_finish(g, phase):
        order = ORDERS[g % 3]
        axis = order[phase]
        fixed = {a: me[a] for a in order[:phase]}
        buf = ra1
        for side, step in ((0, 1), (1, 3)):
            copies["a", phase, g, side].wait_recv()
            fixed[axis] = (me[axis] + step) % 4
            idx = at(g, fixed, side)
            rd[idx] = rd[idx] + buf[g, side]

    def b_start(g, phase):
        order = ORDERS[g % 3]
        axis = order[phase]
        fixed = {a: me[a] for a in order[:phase]}
        buf, send, recv = (rb1, b1_send, b1_recv)
        for side, step in ((0, 1), (1, 3)):
            fixed[axis] = (me[axis] + step) % 4
            copies["b", phase, g, side] = remote(
                rd.at[at(g, fixed)], buf.at[g, side],
                send.at[g, side], recv.at[g, side], device(axis, step),
            )

    def b_finish(g, phase):
        order = ORDERS[g % 3]
        axis = order[phase]
        fixed = {a: me[a] for a in order[:phase]}
        fixed[axis] = me[axis]
        buf = rb1
        for side in (0, 1):
            copies["b", phase, g, side].wait_recv()
        idx = at(g, fixed)
        rd[idx] = rd[idx] + (buf[g, 0] + buf[g, 1])

    def c_start(g, phase):
        order = ORDERS[g % 3]
        axis = order[phase]
        fixed = {a: me[a] for a in order[:phase]}
        buf, send, recv = rb2, b2_send, b2_recv
        for d in (1, 2, 3):
            fixed[axis] = (me[axis] + d) % 4
            copies["c", phase, g, d] = remote(
                rd.at[at(g, fixed)], buf.at[g, d - 1],
                send.at[g, d - 1], recv.at[g, d - 1], device(axis, d),
            )

    def c_finish(g, phase):
        order = ORDERS[g % 3]
        fixed = {a: me[a] for a in order[:phase + 1]}
        buf = rb2
        for d in (1, 2, 3):
            copies["c", phase, g, d].wait_recv()
        return rd[at(g, fixed)] + (buf[g, 0] + (buf[g, 1] + buf[g, 2])), at(g, fixed)

    def pair_finish(g):
        copies["d", g].wait_recv()
        own = halves[g % 4, core].reshape(4, 4, 4, 8, 256)
        rd[SLOT[g]] = rd[SLOT[g]] + own

    for g in range(GROUPS + 3):
        if g < GROUPS:
            product(g)
            pair_start(g)
        if 1 <= g < GROUPS + 1:
            pair_finish(g - 1)
            a_start(g - 1, 0)
        if 3 <= g:
            a_finish(g - 3, 0)
            b_start(g - 3, 0)
        if 7 <= g:
            b_finish(g - 7, 0)
            c_start(g - 7, 1)
    def last_start(o):
        axis = ORDERS[o][2]
        fixed = {a: me[a] for a in ORDERS[o][:2]}
        slots = pl.ds(o * 3, 2 if o == 2 else 3)
        for d in (1, 2, 3):
            fixed[axis] = (me[axis] + d) % 4
            copies["e", o, d] = remote(
                rd.at[at(slots, fixed)], r3.at[d - 1, slots],
                c_send.at[o, d - 1], c_recv.at[o, d - 1], device(axis, d),
            )

    def last_finish(o):
        count = 2 if o == 2 else 3
        slots = pl.ds(o * 3, count)
        for d in (1, 2, 3):
            copies["e", o, d].wait_recv()
        total = rd[slots, x, z, y] + (r3[0, slots] + (r3[1, slots] + r3[2, slots]))
        for i in range(count):
            g = o + 3 * i
            out_ref[g * 8:(g + 1) * 8, :] = total[i] * (1.0 / 16.0)

    for g in range(GROUPS + 2):
        if 4 <= g < GROUPS:
            b_finish(g, 0)
            c_start(g, 1)
        if g >= 2:
            total, index = c_finish(g - 2, 1)
            rd[index] = total
            if g - 2 >= 5:
                last_start((g - 2) % 3)
    for o in (2, 0, 1):
        last_finish(o)
    for n in range(3):
        exchange_sent(n)
    for key, copy in copies.items():
        if key[0] != "d" or key[1] >= GROUPS - 4:
            copy.wait_send()


def shards(items, centroids):
    dma = pltpu.SemaphoreType.DMA
    vmem = pltpu.VMEM
    out, row, col = pl.pallas_call(
        kernel,
        out_shape=(
            jax.ShapeDtypeStruct((64, D), F32),
            jax.ShapeDtypeStruct((1, N), F32),
            jax.ShapeDtypeStruct((8, 8, 128), F32),
        ),
        in_specs=[pl.BlockSpec(memory_space=pltpu.VMEM)] * 2,
        out_specs=[pl.BlockSpec(memory_space=pltpu.VMEM)] * 3,
        scratch_shapes=[
            vmem((8, 128, 8, N), F32),
            vmem((D, N), BF16),
            vmem((8, CHIPS, 8, D), F32),
            vmem((N, N), BF16),
            vmem((N, N), BF16),
            vmem((8, 2, 8, 128), F32),
            vmem((8, 1, 8, 128), F32),
            vmem((8, 1, 8, 128), F32),
            vmem((3, 8, 8, 128), F32),
            vmem((7, 2, 8, 128), F32),
            vmem((7, 1, 8, 128), F32),
            vmem((7, 1, 8, 128), F32),
            vmem((16, 2, 8, 128), F32),
            vmem((16, 1, 8, 128), F32),
            vmem((16, 1, 8, 128), F32),
            vmem((GROUPS, 4, 4, 4, 8, D), F32),
            vmem((GROUPS, 2, 2, 4, 8, D), F32),
            vmem((GROUPS, 2, 4, 4, 8, D), F32),
            vmem((GROUPS, 3, 4, 8, D), F32),
            vmem((3, GROUPS, 8, D), F32),
            vmem((8, N), F32),
            dma((3, 3)), dma((3, 3)),
            dma((GROUPS,)), dma((GROUPS,)),
            dma((GROUPS, 2)), dma((GROUPS, 2)),
            dma((GROUPS, 2)), dma((GROUPS, 2)),
            dma((GROUPS, 3)), dma((GROUPS, 3)),
            dma((3, 3)), dma((3, 3)),
        ],
        compiler_params=pltpu.CompilerParams(
            collective_id=0, has_side_effects=True, vmem_limit_bytes=60 * 2**20
        ),
        name="sinkhorn_step",
    )(items, centroids)
    return out, row.reshape(N), col.transpose(0, 2, 1).reshape(8192)


def solution(mesh):
    return jax.shard_map(
        shards,
        mesh=mesh,
        in_specs=(P(("dp", "mp"), None), P()),
        out_specs=(P(("dp", "mp"), None), P(("dp", "mp")), P()),
        check_vma=False,
    )
```
